128 devices in a mesh: row: 16 (over z, y_hi, core), col: 8 (over x, y_lo).
Axes of the slice: x: 4, y: 4 (y_hi: 2, y_lo: 2; y = y_hi * 2 + y_lo), z: 4, core: 2. Of those that a mesh axis runs over, the one named last changes fastest.
Arguments:
- inputs: bfloat16 [1024, 12288], P('col', 'row'), may hold values from -6 to 6
- weight: bfloat16 [12288, 49152], P('row', 'col'), may hold values from -0.0546875 to 0.0546875
- hidden_bias: float32 [49152], P('col'), may hold values from -4 to 4
- cotangent: bfloat16 [1024, 49152], P('row', 'col'), may hold values from -6 to 6
Outputs:
- activation: bfloat16 [1024, 49152], P('row', 'col')
- input_grad: bfloat16 [1024, 12288], P('col', 'row')
- weight_grad: bfloat16 [12288, 49152], P('row', 'col')
The draws below stay inside these ranges and needn't reach their ends.
All inputs are finite; a program needn't handle non-finite values.
Results may differ from the reference program's by a relative error of at most 0.022.
Values may be sent and summed in bfloat16 or wider, within the bound.
No kernel may reach another device: no remote copies, remote signals or barrier semaphores. Data moves between devices by JAX's collectives and lax.ppermute only.
A program may use at most 192 MiB of HBM per device.

```python
import jax
import jax.numpy as jnp
from jax import lax

D = 12288
FF = 49152
TOKENS = 1024
N_ROW = 16
N_COL = 8


def block_scale(own_key, dims, cuts, least, top_value):
    gain, own = 1.0, jax.random.fold_in(own_key, 6)
    for dim, shards_of in cuts:
        steps = jnp.exp(jax.random.uniform(jax.random.fold_in(own, dim), (shards_of,), jnp.float32, least / len(cuts), top_value / len(cuts)))
        gain = gain * jnp.repeat(steps, dims[dim] // shards_of).reshape([-1 if axis == dim else 1 for axis in range(len(dims))])
    return gain


def noise(own_key, extent, scale, reach, pieces=(), kind=jnp.bfloat16):
    array = jax.random.normal(own_key, extent, jnp.float32) * scale
    if len(pieces) > 0:
        array = block_scale(own_key, extent, pieces, -0.22, 0.18) * array
    return jnp.clip(array, min=-reach, max=reach).astype(kind)


def setup_inputs(seed: int = 0) -> dict:
    splits = jax.random.split(jax.random.key(seed), 5)
    inputs = noise(splits[0], (TOKENS, D), 1.0, 6.0, ((0, 8), (1, 16)))
    weight = noise(splits[1], (D, FF), D ** -0.5, 0.0546875, ((0, 16), (1, 8)))
    hidden_bias = noise(splits[2], (FF,), 1.0, 4.0, ((0, 8),), jnp.float32)
    cotangent = noise(splits[3], (TOKENS, FF), 1.0, 6.0, ((0, 16), (1, 8)))
    return dict(inputs=inputs, weight=weight, hidden_bias=hidden_bias, cotangent=cotangent)


SQRT_TWO_PI = 0.7978845608028654


def gelu_parts(preact):
    cubic = preact * preact * preact
    inner = SQRT_TWO_PI * (preact + 0.044715 * cubic)
    tangent = jnp.tanh(inner)
    activation = 0.5 * preact * (1.0 + tangent)
    slopes = 0.5 * (1.0 + tangent) + 0.5 * preact * (1.0 - tangent * tangent) * SQRT_TWO_PI * (1.0 + 3.0 * 0.044715 * preact * preact)
    return activation, slopes


def reference(inputs, weight, hidden_bias, cotangent):
    width_block = D // N_ROW
    hidden_block = FF // N_COL

    def forward_add(running, index):
        offset = (index * width_block).astype(jnp.int32)
        piece_in = lax.dynamic_slice_in_dim(inputs, offset, width_block, 1)
        piece_w = lax.dynamic_slice_in_dim(weight, offset, width_block, 0)
        partial_sum = jnp.dot(piece_in, piece_w, preferred_element_type=jnp.float32).astype(jnp.bfloat16)
        partial_sum = lax.optimization_barrier(partial_sum)
        return running + partial_sum.astype(jnp.float32), None

    summed, _ = lax.scan(forward_add, jnp.zeros((TOKENS, FF), jnp.float32), jnp.arange(N_ROW, dtype=jnp.int32))
    preact = summed + hidden_bias.astype(jnp.float32)[None, :]
    activation, slopes = gelu_parts(preact)
    grad_hidden = (cotangent.astype(jnp.float32) * slopes).astype(jnp.bfloat16)

    def backward_add(running, index):
        offset = (index * hidden_block).astype(jnp.int32)
        piece_g = lax.dynamic_slice_in_dim(grad_hidden, offset, hidden_block, 1)
        piece_w = lax.dynamic_slice_in_dim(weight, offset, hidden_block, 1)
        partial_sum = lax.dot_general(piece_g, piece_w, (((1,), (1,)), ((), ())), preferred_element_type=jnp.float32).astype(jnp.bfloat16)
        partial_sum = lax.optimization_barrier(partial_sum)
        grad_piece = jnp.dot(inputs.T, piece_g, preferred_element_type=jnp.float32).astype(jnp.bfloat16)
        return running + partial_sum.astype(jnp.float32), grad_piece

    back_sum, grad_pieces = lax.scan(backward_add, jnp.zeros((TOKENS, D), jnp.float32), jnp.arange(N_COL, dtype=jnp.int32))
    weight_grad = grad_pieces.transpose(1, 0, 2).reshape(D, FF)
    return activation.astype(jnp.bfloat16), back_sum.astype(jnp.bfloat16), weight_grad
```

```python
import jax
import jax.numpy as jnp
from jax import lax
from jax.sharding import PartitionSpec as P

SQRT_TWO_PI = 0.7978845608028654
BF16, F32 = jnp.bfloat16, jnp.float32

N_ROW, N_COL = 16, 8
PIECES = 3

PAIRS = {
    "za": lambda z, h, c, x, l: (z ^ 1, h, c, x, l),
    "zb": lambda z, h, c, x, l: (3 - z, h, c, x, l),
    "yh": lambda z, h, c, x, l: (z, 1 - h, c, x, l),
    "xa": lambda z, h, c, x, l: (z, h, c, x ^ 1, l),
    "xb": lambda z, h, c, x, l: (z, h, c, 3 - x, l),
    "yl": lambda z, h, c, x, l: (z, h, c, x, 1 - l),
    "core": lambda z, h, c, x, l: (z, h, 1 - c, x, l),
}
ROW_ORDERS = (("za", "zb", "yh"), ("zb", "yh", "za"), ("yh", "za", "zb"))
COL_ORDERS = (("xa", "xb", "yl"), ("xb", "yl", "xa"), ("yl", "xa", "xb"))


def pairing(dim):
    pairs = []
    for device in range(N_ROW * N_COL):
        row, col = divmod(device, N_COL)
        z, h, c, x, l = PAIRS[dim](row // 4, row // 2 % 2, row % 2, col // 2, col % 2)
        pairs.append((device, ((z * 2 + h) * 2 + c) * N_COL + x * 2 + l))
    return pairs


def swap(array, dim):
    return lax.ppermute(array, ("row", "col"), pairing(dim))


def gather_rounds(blocks, orders):
    for turn in (2, 1, 0):
        others = [swap(block, order[turn]) for block, order in zip(blocks, orders)]
        blocks = [jnp.concatenate(pair, axis=0) for pair in zip(blocks, others)]
    return blocks


def scatter_rounds(blocks, orders):
    for turn in range(3):
        halves = [block.shape[0] // 2 for block in blocks]
        others = [swap(block[half:], order[turn]) for block, half, order in zip(blocks, halves, orders)]
        blocks = [
            (block[:half].astype(F32) + other.astype(F32)).astype(BF16)
            for block, half, other in zip(blocks, halves, others)
        ]
    return blocks


def reorder(array, source, target):
    cube = array.reshape(2, 2, 2, array.shape[0] // 8, array.shape[1])
    cube = cube.transpose([source.index(dim) for dim in target] + [3, 4])
    return cube.reshape(array.shape)


def flip(array, bits):
    blocks = array.reshape(8, array.shape[0] // 8, array.shape[1])
    return jnp.take(blocks, jnp.arange(8) ^ bits, axis=0).reshape(array.shape)


def gelu_parts(preact):
    cubic = preact * preact * preact
    inner = SQRT_TWO_PI * (preact + 0.044715 * cubic)
    tangent = jnp.tanh(inner)
    activation = 0.5 * preact * (1.0 + tangent)
    slopes = 0.5 * (1.0 + tangent) + 0.5 * preact * (1.0 - tangent * tangent) * SQRT_TWO_PI * (
        1.0 + 3.0 * 0.044715 * preact * preact
    )
    return (activation, slopes)


def halves(array, core):
    width = array.shape[-1] // 2
    cut = lambda which: lax.dynamic_slice_in_dim(array, which * width, width, array.ndim - 1)
    return cut(core), cut(1 - core)


def joined(mine, others, core, axis):
    return jnp.where(
        core == 0, jnp.concatenate([mine, others], axis), jnp.concatenate([others, mine], axis)
    )


def body(inputs, weight, hidden_bias, cotangent):
    row, col = lax.axis_index("row"), lax.axis_index("col")
    core = row % 2
    z, x = row // 4, col // 2
    cube = lambda ring, last: ((ring % 2) ^ (ring // 2)) * 4 + ring // 2 * 2 + last
    bits = cube(z, row // 2 % 2) ^ cube(x, col % 2)
    base = ROW_ORDERS[0]

    weight_mine, weight_sent = halves(weight, core)
    weight_other = swap(weight_sent, "core")
    cot_mine, cot_sent = halves(cotangent, core)
    cot = joined(cot_mine, swap(cot_sent, "core"), core, 0)
    bias, _ = halves(hidden_bias[None, :], core)

    third = inputs.shape[1] // 3
    gathered = gather_rounds([inputs[:, i * third : (i + 1) * third] for i in range(3)], COL_ORDERS)
    tokens = flip(
        jnp.concatenate([reorder(g, o, COL_ORDERS[0]) for g, o in zip(gathered, COL_ORDERS)], axis=1), bits
    )
    tokens_other = swap(tokens, "core")

    orders = [ROW_ORDERS[i % 3] for i in range(PIECES)]
    width = weight.shape[1] // 2 // PIECES
    cols = [slice(i * width, (i + 1) * width) for i in range(PIECES)]
    mine = [reorder(tokens, base, order) for order in orders]
    other = [reorder(tokens_other, base, order) for order in orders]

    partials = [
        (
            jnp.dot(mine[i], weight_mine[:, cols[i]], preferred_element_type=F32)
            + jnp.dot(other[i], weight_other[:, cols[i]], preferred_element_type=F32)
        ).astype(BF16)
        for i in range(PIECES)
    ]
    summed = scatter_rounds(partials, orders)
    acts, grads = [], []
    for i in range(PIECES):
        act, slopes = gelu_parts(summed[i].astype(F32) + bias[:, cols[i]])
        acts.append(act.astype(BF16))
        grads.append((cot[:, cols[i]].astype(F32) * slopes).astype(BF16))
    act = jnp.concatenate(acts, axis=1)
    tall = act.shape[0] // 2
    act_mine = lax.dynamic_slice_in_dim(act, core * tall, tall, 0)
    act_sent = lax.dynamic_slice_in_dim(act, (1 - core) * tall, tall, 0)
    activation = joined(act_mine, swap(act_sent, "core"), core, 1)

    grads = gather_rounds(grads, orders)
    grads_other = [swap(grad, "core") for grad in grads]
    back = jnp.zeros(tokens.shape, F32)
    pieces_mine, pieces_other = [], []
    for i in range(PIECES):
        sent = weight_sent[:, cols[i]]
        term = lax.dot_general(grads[i], weight_mine[:, cols[i]], (((1,), (1,)), ((), ())), preferred_element_type=F32)
        term += lax.dot_general(grads_other[i], sent, (((1,), (1,)), ((), ())), preferred_element_type=F32)
        back += reorder(term, orders[i], base)
        for grad, pieces in ((grads[i], pieces_mine), (grads_other[i], pieces_other)):
            pieces.append(
                lax.dot_general(mine[i], grad, (((0,), (0,)), ((), ())), preferred_element_type=F32).astype(BF16)
            )
    weight_grad = joined(jnp.concatenate(pieces_mine, 1), jnp.concatenate(pieces_other, 1), core, 1)

    back = flip(back.astype(BF16), bits)
    back = scatter_rounds(
        [reorder(back[:, i * third : (i + 1) * third], COL_ORDERS[0], COL_ORDERS[i]) for i in range(3)], COL_ORDERS
    )
    return (activation, jnp.concatenate(back, axis=1), weight_grad)


def solution(mesh):
    return jax.shard_map(
        body,
        mesh=mesh,
        in_specs=(P("col", "row"), P("row", "col"), P("col"), P("row", "col")),
        out_specs=(P("row", "col"), P("col", "row"), P("row", "col")),
        check_vma=False,
    )
```

```python
import math

import jax
import jax.numpy as jnp
from jax import lax
from jax.experimental import pallas as pl
from jax.experimental.pallas import tpu as pltpu
from jax.sharding import PartitionSpec as P

SQRT_TWO_PI = 0.7978845608028654
BF16, F32 = jnp.bfloat16, jnp.float32

N_ROW, N_COL = 16, 8
PIECES = 6
BLOCKS = 8
SPARE = 4 * 2**20

PAIRS = {
    "za": lambda z, h, c, x, l: (z ^ 1, h, c, x, l),
    "zb": lambda z, h, c, x, l: (3 - z, h, c, x, l),
    "yh": lambda z, h, c, x, l: (z, 1 - h, c, x, l),
    "xa": lambda z, h, c, x, l: (z, h, c, x ^ 1, l),
    "xb": lambda z, h, c, x, l: (z, h, c, 3 - x, l),
    "yl": lambda z, h, c, x, l: (z, h, c, x, 1 - l),
    "core": lambda z, h, c, x, l: (z, h, 1 - c, x, l),
}
ROW_DIMS, COL_DIMS = ("za", "zb", "yh"), ("xa", "xb", "yl")
ROW_ORDERS = (("za", "zb", "yh"), ("zb", "yh", "za"), ("yh", "za", "zb"))
COL_ORDERS = (("xa", "xb", "yl"), ("xb", "yl", "xa"), ("yl", "xa", "xb"))

WHOLE = pl.BlockSpec(memory_space=pltpu.VMEM)
UNREAD = pl.BlockSpec(memory_space=pl.ANY)
SCALAR = pl.BlockSpec(memory_space=pltpu.SMEM)


def pairing(dim):
    pairs = []
    for device in range(N_ROW * N_COL):
        row, col = divmod(device, N_COL)
        z, h, c, x, l = PAIRS[dim](row // 4, row // 2 % 2, row % 2, col // 2, col % 2)
        pairs.append((device, ((z * 2 + h) * 2 + c) * N_COL + x * 2 + l))
    return pairs


def swap(array, dim):
    return lax.ppermute(array, ("row", "col"), pairing(dim))


def place(block, dims, order):
    spot = 0
    for dim in order:
        spot = spot * 2 + ((block >> (len(dims) - 1 - dims.index(dim))) & 1)
    return spot


def local_call(kernel, out_shape, operands, specs, deps=(), flops=0, moved=0, name=None, **kw):
    n = len(operands)

    def run(*refs):
        kernel(*refs[:n], *refs[n + len(deps) :])

    moved = moved or sum(a.size * a.dtype.itemsize for a in operands)
    outs = out_shape if isinstance(out_shape, list) else [out_shape]
    held = sum(math.prod(a.shape) * a.dtype.itemsize for a in list(operands) + outs)
    return pl.pallas_call(
        run,
        out_shape=out_shape,
        in_specs=list(specs) + [UNREAD] * len(deps),
        out_specs=[WHOLE] * len(out_shape) if isinstance(out_shape, list) else WHOLE,
        compiler_params=pltpu.CompilerParams(vmem_limit_bytes=held + SPARE),
        cost_estimate=pl.CostEstimate(flops=flops, bytes_accessed=moved, transcendentals=0),
        name=name,
        **kw,
    )(*operands, *deps)


def shape(*dims, dtype=BF16):
    return jax.ShapeDtypeStruct(dims, dtype)


def near_shape(*dims, dtype=BF16):
    return pltpu.VMEM(dims, dtype)


def in_hbm(array):
    return pltpu.with_memory_space_constraint(array, pltpu.HBM)


def gather_round(blocks, orders, turn):
    others = [swap(block, order[turn]) for block, order in zip(blocks, orders)]
    return [jnp.concatenate(pair, axis=0) for pair in zip(blocks, others)]


def stack(near, far, deps):
    tall = near.shape[0]

    def kernel(near_ref, far_ref, out):
        out[:tall, :] = near_ref[...]
        out[tall:, :] = far_ref[...]

    return local_call(kernel, near_shape(2 * tall, near.shape[1]), [near, far], [WHOLE] * 2, deps, name="stack")


def join(arrays, deps):
    tall, width = arrays[0].shape

    def kernel(*refs):
        for i, ref in enumerate(refs[:-1]):
            refs[-1][i * tall : (i + 1) * tall, :] = ref[...]

    out_shape = near_shape(len(arrays) * tall, width)
    return local_call(kernel, out_shape, arrays, [WHOLE] * len(arrays), deps, name="join")


def other_half(core, array, width, offset, deps):
    rows, tile = array.shape[0], 512
    reach, first = array.shape[1] // 2 // tile, offset // tile

    def kernel(core_ref, block_ref, *refs):
        refs[-1][...] = block_ref[...]

    return pl.pallas_call(
        kernel,
        out_shape=shape(rows, width),
        grid_spec=pltpu.PrefetchScalarGridSpec(
            num_scalar_prefetch=1,
            grid=(width // tile,),
            in_specs=[pl.BlockSpec((rows, tile), lambda j, core_ref: (0, (1 - core_ref[0]) * reach + first + j))]
            + [UNREAD] * len(deps),
            out_specs=pl.BlockSpec((rows, tile), lambda j, core_ref: (0, j)),
        ),
        compiler_params=pltpu.CompilerParams(vmem_limit_bytes=8 * 2**20),
        cost_estimate=pl.CostEstimate(flops=0, bytes_accessed=4 * rows * width, transcendentals=0),
        name="other_half",
    )(core, in_hbm(array), *deps)


def order_tokens(bits, parts):
    tall, wide = parts[0].shape[0] // BLOCKS, parts[0].shape[1]

    def kernel(bits_ref, *refs):
        *part_refs, out = refs
        for block in range(BLOCKS):
            source = block ^ bits_ref[0]
            for i, part in enumerate(part_refs):
                spot = pl.multiple_of(place(source, COL_DIMS, COL_ORDERS[i]) * tall, tall)
                out[block * tall : (block + 1) * tall, i * wide : (i + 1) * wide] = part[pl.ds(spot, tall), :]

    out_shape = near_shape(BLOCKS * tall, wide * len(parts))
    return local_call(kernel, out_shape, [bits] + parts, [SCALAR] + [WHOLE] * len(parts), name="order_tokens")


def transposed(tokens, deps):
    tall = tokens.shape[0] // BLOCKS

    def kernel(tokens_ref, *outs):
        for block in range(BLOCKS):
            flipped = tokens_ref[block * tall : (block + 1) * tall, :].T
            for order, out in zip(ROW_ORDERS, outs):
                spot = place(block, ROW_DIMS, order) * tall
                out[:, spot : spot + tall] = flipped

    out_shape = [near_shape(tokens.shape[1], tokens.shape[0])] * 3
    return local_call(kernel, out_shape, [tokens], [WHOLE], deps, name="transposed")


def project(core, mine, other, weight, weight_other, piece, first, width, deps):
    tokens, model = mine.shape
    half, tall = tokens // 2, tokens // BLOCKS
    order = ROW_ORDERS[piece % 3]
    tile = 256
    reach, steps = weight.shape[1] // 2 // tile, width // tile

    def kernel(core_ref, mine_ref, other_ref, near_ref, far_ref, *refs):
        send, keep = refs[-2:]
        for chunk in range(2):
            rows = slice(chunk * half, (chunk + 1) * half)
            total = jnp.dot(mine_ref[rows, :], near_ref[...], preferred_element_type=F32)
            total += jnp.dot(other_ref[rows, :], far_ref[...], preferred_element_type=F32)
            total = total.astype(BF16)
            for i in range(4):
                spot = place(chunk * 4 + i, ROW_DIMS, order)
                target = send if spot >= 4 else keep
                target[spot % 4 * tall : (spot % 4 + 1) * tall, :] = total[i * tall : (i + 1) * tall]

    return pl.pallas_call(
        kernel,
        out_shape=[near_shape(half, width)] * 2,
        grid_spec=pltpu.PrefetchScalarGridSpec(
            num_scalar_prefetch=1,
            grid=(steps,),
            in_specs=[
                WHOLE,
                WHOLE,
                pl.BlockSpec((model, tile), lambda j, core_ref: (0, core_ref[0] * reach + piece * steps + j)),
                pl.BlockSpec((model, tile), lambda j, core_ref: (0, (piece - first) * steps + j)),
            ]
            + [UNREAD] * len(deps),
            out_specs=[pl.BlockSpec((half, tile), lambda j, core_ref: (0, j))] * 2,
        ),
        compiler_params=pltpu.CompilerParams(vmem_limit_bytes=10 * 2**20),
        cost_estimate=pl.CostEstimate(flops=4 * tokens * model * width, bytes_accessed=1, transcendentals=0),
        name="project",
    )(core, mine, other, in_hbm(weight), in_hbm(weight_other), *deps)


def add_halves(keep, received, deps):
    half = keep.shape[0] // 2

    def kernel(keep_ref, received_ref, send, kept):
        total = (keep_ref[...].astype(F32) + received_ref[...].astype(F32)).astype(BF16)
        kept[...] = total[:half]
        send[...] = total[half:]

    out_shape = [near_shape(half, keep.shape[1])] * 2
    return local_call(kernel, out_shape, [keep, received], [WHOLE] * 2, deps, name="add_halves")


def gelu_parts(preact):
    cubic = preact * preact * preact
    inner = SQRT_TWO_PI * (preact + 0.044715 * cubic)
    tangent = jnp.tanh(inner)
    activation = 0.5 * preact * (1.0 + tangent)
    slopes = 0.5 * (1.0 + tangent) + 0.5 * preact * (1.0 - tangent * tangent) * SQRT_TWO_PI * (
        1.0 + 3.0 * 0.044715 * preact * preact
    )
    return (activation, slopes)


def activate(core, keep, received, bias, cot, cot_other, piece, deps):
    tall, width = keep.shape
    half, reach = tall // 2, cot.shape[1] // 2

    def kernel(core_ref, keep_ref, received_ref, bias_ref, cot_ref, cot_other_ref, grad, act_mine, act_sent):
        cols = pl.ds(pl.multiple_of(core_ref[0] * reach + piece * width, 128), width)
        there = slice(piece * width, (piece + 1) * width)
        sides = ((core_ref[0], act_mine, cot_ref[:, cols]), (1 - core_ref[0], act_sent, cot_other_ref[:, there]))
        for owner, act_ref, slope_cot in sides:
            rows = pl.ds(pl.multiple_of(owner * half, half), half)
            preact = keep_ref[rows, :].astype(F32) + received_ref[rows, :].astype(F32) + bias_ref[:, cols]
            act, slopes = gelu_parts(preact)
            grad[rows, :] = (slope_cot.astype(F32) * slopes).astype(BF16)
            act_ref[...] = act.astype(BF16)

    return local_call(
        kernel,
        [near_shape(tall, width), near_shape(half, width), near_shape(half, width)],
        [core, keep, received, bias, cot, cot_other],
        [SCALAR] + [WHOLE] * 5,
        deps,
        name="activate",
    )


def place_activation(core, mine, other, deps):
    rows, width = mine[0].shape
    reach = len(mine) * width

    def kernel(core_ref, *refs):
        *mine_refs, other_ref, out = refs
        for i, ref in enumerate(mine_refs):
            out[:, pl.ds(pl.multiple_of(core_ref[0] * reach + i * width, 128), width)] = ref[...]
            there = pl.ds(pl.multiple_of((1 - core_ref[0]) * reach + i * width, 128), width)
            out[:, there] = other_ref[i * rows : (i + 1) * rows, :]

    return local_call(
        kernel,
        shape(rows, 2 * reach),
        [core, *mine, other],
        [SCALAR] + [WHOLE] * (len(mine) + 1),
        deps,
        name="place_activation",
    )


def index_of(array, arrays):
    return [array is other for other in arrays].index(True)


def distinct(arrays):
    found = []
    for array in arrays:
        if not any(array is other for other in found):
            found.append(array)
    return found


def input_terms(core, weight, tokens, total, grads, deps, bits=None):
    keys = list(grads)
    arrays = distinct(array for sides in grads.values() for array, _ in sides.values())
    half, width = tokens // 2, arrays[0].shape[1]
    tall = half * 2 // BLOCKS
    model, reach = weight.shape[0], weight.shape[1] // 2 // width
    started, last = total is not None, bits is not None
    third = model // 3
    n_in = started + len(arrays)

    def kernel(core_ref, bits_ref, weight_ref, *refs):
        ins, outs = list(refs[:n_in]), refs[n_in + len(deps) :]
        acc = outs[-1]
        total_ref = ins.pop(0) if started else None

        @pl.when(pl.program_id(0) == 0)
        def _():
            acc[...] = total_ref[...] if started else jnp.zeros(acc.shape, F32)

        for step, key in enumerate(keys):

            @pl.when(pl.program_id(0) == step)
            def _():
                for side, (array, row) in grads[key].items():
                    ref = ins[index_of(array, arrays)]
                    term = lax.dot_general(
                        ref[row : row + half, :], weight_ref[...], (((1,), (1,)), ((), ())), preferred_element_type=F32
                    )
                    for i in range(4):
                        spot = place(side * 4 + i, ROW_ORDERS[key[0] % 3], ROW_DIMS)
                        acc[spot * tall : (spot + 1) * tall, :] += term[i * tall : (i + 1) * tall]

        if last:

            @pl.when(pl.program_id(0) == len(keys) - 1)
            def _():
                for block in range(BLOCKS):
                    source = pl.multiple_of((block ^ bits_ref[0]) * tall, tall)
                    rows = acc[pl.ds(source, tall), :].astype(BF16)
                    for i, order in enumerate(COL_ORDERS):
                        spot = place(block, COL_DIMS, order)
                        target = outs[i * 2 if spot >= 4 else i * 2 + 1]
                        target[spot % 4 * tall : (spot % 4 + 1) * tall, :] = rows[:, i * third : (i + 1) * third]

    def column(step, core_ref, bits_ref):
        owner, piece = core_ref[0], 0
        for i, (p, far) in enumerate(keys):
            piece = jnp.where(step == i, p, piece)
            owner = jnp.where(step == i, 1 - core_ref[0] if far else core_ref[0], owner)
        return (0, owner * reach + piece)

    return pl.pallas_call(
        kernel,
        out_shape=[near_shape(half, third)] * 6 if last else [near_shape(2 * half, model, dtype=F32)],
        grid_spec=pltpu.PrefetchScalarGridSpec(
            num_scalar_prefetch=2,
            grid=(len(keys),),
            in_specs=[pl.BlockSpec((model, width), column)] + [WHOLE] * n_in + [UNREAD] * len(deps),
            out_specs=[WHOLE] * (6 if last else 1),
            scratch_shapes=[pltpu.VMEM((2 * half, model), F32)] if last else [],
        ),
        compiler_params=pltpu.CompilerParams(vmem_limit_bytes=24 * 2**20),
        cost_estimate=pl.CostEstimate(
            flops=2 * half * width * model * sum(map(len, grads.values())), bytes_accessed=1, transcendentals=0
        ),
        name="input_terms",
    )(core, bits if last else core, in_hbm(weight), *([total] if started else []), *arrays, *deps)


def weight_terms(core, flipped, grads, so_far, cols, deps):
    keys = list(grads)
    arrays = distinct(array for sides in grads.values() for array, _ in sides.values())
    model, tokens = flipped[0].shape
    half, width = tokens // 2, arrays[0].shape[1]
    reach = cols // 2 // width
    aliased = so_far is not None
    n_deps = len(deps)

    def kernel(core_ref, *refs):
        flipped_refs, grad_refs, out = refs[:3], refs[3 : 3 + len(arrays)], refs[-1]
        for step, (piece, _) in enumerate(keys):

            @pl.when(pl.program_id(0) == step)
            def _():
                left = flipped_refs[piece % 3]
                total = 0.0
                for side, (array, row) in grads[keys[step]].items():
                    right = grad_refs[index_of(array, arrays)][row : row + half, :]
                    total += jnp.dot(left[:, side * half : (side + 1) * half], right, preferred_element_type=F32)
                out[...] = total.astype(BF16)

    def column(step, core_ref):
        owner, piece = core_ref[0], 0
        for i, (p, far) in enumerate(keys):
            hit = step == i
            piece = jnp.where(hit, p, piece)
            owner = jnp.where(hit, 1 - core_ref[0] if far else core_ref[0], owner)
        return (0, owner * reach + piece)

    operands = [core, *flipped, *arrays] + list(deps) + ([in_hbm(so_far)] if aliased else [])
    return pl.pallas_call(
        kernel,
        out_shape=shape(model, cols),
        grid_spec=pltpu.PrefetchScalarGridSpec(
            num_scalar_prefetch=1,
            grid=(len(keys),),
            in_specs=[WHOLE] * (3 + len(arrays)) + [UNREAD] * (n_deps + aliased),
            out_specs=pl.BlockSpec((model, width), column),
        ),
        input_output_aliases={len(operands) - 1: 0} if aliased else {},
        compiler_params=pltpu.CompilerParams(vmem_limit_bytes=24 * 2**20),
        cost_estimate=pl.CostEstimate(
            flops=2 * model * tokens * width * len(keys), bytes_accessed=1, transcendentals=0
        ),
        name="weight_terms",
    )(*operands)


def after(arrays, *deps):
    return list(lax.optimization_barrier((tuple(arrays), deps))[0])


def body(inputs, weight, hidden_bias, cotangent):
    row, col = lax.axis_index("row"), lax.axis_index("col")
    core = (row % 2).astype(jnp.int32)[None]
    cube = lambda ring, last: ((ring % 2) ^ (ring // 2)) * 4 + ring // 2 * 2 + last
    bits = (cube(row // 4, row // 2 % 2) ^ cube(col // 2, col % 2)).astype(jnp.int32)[None]
    hidden = weight.shape[1]
    width = hidden // 2 // PIECES
    sets = (range(0, 3), range(3, 6))
    bias = hidden_bias[None, :]

    third = inputs.shape[1] // 3
    parts = [inputs[:, i * third : (i + 1) * third] for i in range(3)]
    weight_other = []
    for turn in (2, 1, 0):
        parts = after(gather_round(parts, COL_ORDERS, turn))
        if turn > 0:
            sent = other_half(core, weight, 3 * width, (2 - turn) * 3 * width, parts)
            weight_other.append(swap(sent, "core"))
    parts_other = [swap(part, "core") for part in parts]
    mine = order_tokens(bits, parts)
    other = order_tokens(bits, parts_other)

    orders = [ROW_ORDERS[p % 3] for p in range(PIECES)]
    send, keep, last = [None] * PIECES, [None] * PIECES, ()
    for p in range(PIECES):
        group = p // 3
        send[p], keep[p] = project(core, mine, other, weight, weight_other[group], p, 3 * group, width, last)
        last = (keep[p],)
    cot_other = swap(other_half(core, cotangent, hidden // 2, 0, last), "core")

    received = [None] * PIECES
    for turn in range(3):
        for p in range(PIECES):
            received[p] = swap(send[p], orders[p][turn])
        if turn < 2:
            for p in range(PIECES):
                send[p], keep[p] = add_halves(keep[p], received[p], last)
                last = (keep[p],)
    grads, act_mine, act_sent = [], [], []
    for p in range(PIECES):
        grad, a, b = activate(core, keep[p], received[p], bias, cotangent, cot_other, p, last)
        last = (grad,)
        grads.append(grad)
        act_mine.append(a)
        act_sent.append(b)

    for turn in (2, 1):
        received = [swap(grads[p], orders[p][turn]) for p in range(PIECES)]
        for p in range(PIECES):
            grads[p] = stack(grads[p], received[p], last)
            last = (grads[p],)
    tokens = mine.shape[0]
    half = tokens // 2
    pieces = {}

    def hold(group, side, arrays, deps):
        both = join(arrays, deps)
        there = swap(both, "core")
        for i, p in enumerate(group):
            pieces[p, 0, side] = (arrays[i], 0)
            pieces[p, 1, side] = (there, i * half)
        return both

    def terms(group, sides, cores=(0, 1)):
        return {(p, far): {side: pieces[p, far, side] for side in sides} for p in group for far in cores}

    first, second = sets
    arrived = {p: swap(grads[p], orders[p][0]) for p in first}
    hold(first, 0, [grads[p] for p in first], last)
    hold(second, 0, [grads[p] for p in second], last)
    flipped = transposed(mine, last)
    (total,) = input_terms(core, weight, tokens, None, terms(first, (0,)), (flipped[0],))
    (total,) = input_terms(core, weight, tokens, total, terms(second, (0,)), ())
    sends = after([grads[p] for p in second], total)
    arrived |= {p: swap(sends[i], orders[p][0]) for i, p in enumerate(second)}
    ready = after([arrived[p] for p in first], sends[0])
    hold(first, 1, ready, (total,))
    (total,) = input_terms(core, weight, tokens, total, terms(first, (1,), (0,)), ())
    (total,) = input_terms(core, weight, tokens, total, terms(first, (1,), (1,)), ())
    weight_grad = weight_terms(core, flipped, terms(first, (0, 1)), None, hidden, (total,))
    act_other = swap(join(act_sent, (total,)), "core")
    ready = after([arrived[p] for p in second], total)
    hold(second, 1, ready, (total,))
    (total,) = input_terms(core, weight, tokens, total, terms(second, (1,), (0,)), (in_hbm(weight_grad),))
    back = input_terms(core, weight, tokens, total, terms(second, (1,), (1,)), (), bits=bits)

    send, keep, last = back[0::2], back[1::2], ()
    for turn in range(3):
        received = [swap(s, order[turn]) for s, order in zip(send, COL_ORDERS)]
        if turn == 0:
            weight_grad = weight_terms(core, flipped, terms(second, (0, 1)), weight_grad, hidden, (back[1],))
            last = (in_hbm(weight_grad),)
        if turn < 2:
            pairs = [add_halves(k, r, last) for k, r in zip(keep, received)]
            send, keep, last = [a for a, _ in pairs], [b for _, b in pairs], ()
    activation = place_activation(core, act_mine, act_other, (keep[0],))
    input_grad = jnp.concatenate(
        [(k.astype(F32) + r.astype(F32)).astype(BF16) for k, r in zip(keep, received)], axis=1
    )
    return (activation, input_grad, weight_grad)


def solution(mesh):
    return jax.shard_map(
        body,
        mesh=mesh,
        in_specs=(P("col", "row"), P("row", "col"), P("col"), P("row", "col")),
        out_specs=(P("row", "col"), P("col", "row"), P("row", "col")),
        check_vma=False,
    )
```

```python
import math

import jax
import jax.numpy as jnp
from jax import lax
from jax.experimental import pallas as pl
from jax.experimental.pallas import tpu as pltpu
from jax.sharding import PartitionSpec as P

SQRT_TWO_PI = 0.7978845608028654
BF16, F32 = jnp.bfloat16, jnp.float32

N_ROW, N_COL = 16, 8
PIECES = 6
BLOCKS = 8
SPARE = 4 * 2**20

PAIRS = {
    "za": lambda z, h, c, x, l: (z ^ 1, h, c, x, l),
    "zb": lambda z, h, c, x, l: (3 - z, h, c, x, l),
    "yh": lambda z, h, c, x, l: (z, 1 - h, c, x, l),
    "xa": lambda z, h, c, x, l: (z, h, c, x ^ 1, l),
    "xb": lambda z, h, c, x, l: (z, h, c, 3 - x, l),
    "yl": lambda z, h, c, x, l: (z, h, c, x, 1 - l),
    "core": lambda z, h, c, x, l: (z, h, 1 - c, x, l),
}
ROW_DIMS, COL_DIMS = ("za", "zb", "yh"), ("xa", "xb", "yl")
ROW_ORDERS = (("za", "zb", "yh"), ("zb", "yh", "za"), ("yh", "za", "zb"))
COL_ORDERS = (("xa", "xb", "yl"), ("xb", "yl", "xa"), ("yl", "xa", "xb"))

WHOLE = pl.BlockSpec(memory_space=pltpu.VMEM)
UNREAD = pl.BlockSpec(memory_space=pl.ANY)
SCALAR = pl.BlockSpec(memory_space=pltpu.SMEM)
LIGHT = pl.CostEstimate(flops=0, bytes_accessed=1, transcendentals=0)


def pairing(dim):
    pairs = []
    for device in range(N_ROW * N_COL):
        row, col = divmod(device, N_COL)
        z, h, c, x, l = PAIRS[dim](row // 4, row // 2 % 2, row % 2, col // 2, col % 2)
        pairs.append((device, ((z * 2 + h) * 2 + c) * N_COL + x * 2 + l))
    return pairs


def swap(array, dim):
    return lax.ppermute(array, ("row", "col"), pairing(dim))


def place(block, dims, order):
    spot = 0
    for dim in order:
        spot = spot * 2 + ((block >> (len(dims) - 1 - dims.index(dim))) & 1)
    return spot


def local_call(kernel, out_shape, operands, specs, deps=(), name=None, **kw):
    n = len(operands)

    def run(*refs):
        kernel(*refs[:n], *refs[n + len(deps) :])

    outs = out_shape if isinstance(out_shape, list) else [out_shape]
    held = sum(math.prod(a.shape) * a.dtype.itemsize for a in list(operands) + outs)
    return pl.pallas_call(
        run,
        out_shape=out_shape,
        in_specs=list(specs) + [UNREAD] * len(deps),
        out_specs=[WHOLE] * len(out_shape) if isinstance(out_shape, list) else WHOLE,
        compiler_params=pltpu.CompilerParams(vmem_limit_bytes=held + SPARE),
        cost_estimate=LIGHT,
        name=name,
        **kw,
    )(*operands, *deps)


def shape(*dims, dtype=BF16):
    return jax.ShapeDtypeStruct(dims, dtype)


def near_shape(*dims, dtype=BF16):
    return pltpu.VMEM(dims, dtype)


def in_hbm(array):
    return pltpu.with_memory_space_constraint(array, pltpu.HBM)


def gather_round(blocks, orders, turn):
    others = [swap(block, order[turn]) for block, order in zip(blocks, orders)]
    return [jnp.concatenate(pair, axis=0) for pair in zip(blocks, others)]


def stack(near, far, deps):
    tall = near.shape[0]

    def kernel(near_ref, far_ref, out):
        out[:tall, :] = near_ref[...]
        out[tall:, :] = far_ref[...]

    return local_call(kernel, near_shape(2 * tall, near.shape[1]), [near, far], [WHOLE] * 2, deps, name="stack")


def join(arrays, deps):
    tall, width = arrays[0].shape

    def kernel(*refs):
        for i, ref in enumerate(refs[:-1]):
            refs[-1][i * tall : (i + 1) * tall, :] = ref[...]

    out_shape = near_shape(len(arrays) * tall, width)
    return local_call(kernel, out_shape, arrays, [WHOLE] * len(arrays), deps, name="join")


def take_halves(core, weights, deps):
    n = len(weights)
    model, reach = weights[0].shape[0], weights[0].shape[1] // 2

    def kernel(core_ref, *refs):
        outs, sems = refs[-1 - n : -1], refs[-1]
        start = pl.multiple_of(core_ref[0] * reach, reach)
        copies = [
            pltpu.make_async_copy(ref.at[:, pl.ds(start, reach)], out, sems.at[i])
            for i, (ref, out) in enumerate(zip(refs[:n], outs))
        ]
        for copy in copies:
            copy.start()
        for copy in copies:
            copy.wait()

    return pl.pallas_call(
        kernel,
        out_shape=[near_shape(model, reach)] * n,
        in_specs=[SCALAR] + [UNREAD] * (n + len(deps)),
        out_specs=[WHOLE] * n,
        scratch_shapes=[pltpu.SemaphoreType.DMA((n,))],
        compiler_params=pltpu.CompilerParams(vmem_limit_bytes=12 * 2**20),
        cost_estimate=LIGHT,
        name="take_halves",
    )(core, *[in_hbm(weight) for weight in weights], *deps)


def order_tokens(bits, parts, deps):
    tall, wide = parts[0].shape[0] // BLOCKS, parts[0].shape[1]

    def kernel(bits_ref, *refs):
        *part_refs, out = refs
        for block in range(BLOCKS):
            source = block ^ bits_ref[0]
            for i, part in enumerate(part_refs):
                spot = pl.multiple_of(place(source, COL_DIMS, COL_ORDERS[i]) * tall, tall)
                out[block * tall : (block + 1) * tall, i * wide : (i + 1) * wide] = part[pl.ds(spot, tall), :]

    out_shape = near_shape(BLOCKS * tall, wide * len(parts))
    return local_call(kernel, out_shape, [bits] + parts, [SCALAR] + [WHOLE] * len(parts), deps, name="order_tokens")


def transposed(tokens, deps):
    tall = tokens.shape[0] // BLOCKS

    def kernel(tokens_ref, *outs):
        for block in range(BLOCKS):
            flipped = tokens_ref[block * tall : (block + 1) * tall, :].T
            for order, out in zip(ROW_ORDERS, outs):
                spot = place(block, ROW_DIMS, order) * tall
                out[:, spot : spot + tall] = flipped

    out_shape = [near_shape(tokens.shape[1], tokens.shape[0])] * 3
    return local_call(kernel, out_shape, [tokens], [WHOLE], deps, name="transposed")


def project(mine, other, weight, weight_other, piece, width, deps):
    tokens = mine.shape[0]
    half, tall = tokens // 2, tokens // BLOCKS
    order = ROW_ORDERS[piece % 3]
    cols = slice(piece * width, (piece + 1) * width)

    def kernel(mine_ref, other_ref, near_ref, far_ref, send, keep):
        right = jnp.concatenate([near_ref[:, cols], far_ref[:, cols]], axis=0)
        for chunk in range(2):
            rows = slice(chunk * half, (chunk + 1) * half)
            left = jnp.concatenate([mine_ref[rows, :], other_ref[rows, :]], axis=1)
            total = jnp.dot(left, right, preferred_element_type=F32).astype(BF16)
            for i in range(4):
                spot = place(chunk * 4 + i, ROW_DIMS, order)
                target = send if spot >= 4 else keep
                target[spot % 4 * tall : (spot % 4 + 1) * tall, :] = total[i * tall : (i + 1) * tall]

    return local_call(
        kernel,
        [near_shape(half, width)] * 2,
        [mine, other, weight, weight_other],
        [WHOLE] * 4,
        deps,
        name="project",
    )


def add_halves(keep, received, deps):
    half = keep.shape[0] // 2

    def kernel(keep_ref, received_ref, send, kept):
        total = (keep_ref[...].astype(F32) + received_ref[...].astype(F32)).astype(BF16)
        kept[...] = total[:half]
        send[...] = total[half:]

    out_shape = [near_shape(half, keep.shape[1])] * 2
    return local_call(kernel, out_shape, [keep, received], [WHOLE] * 2, deps, name="add_halves")


def gelu_parts(preact):
    cubic = preact * preact * preact
    inner = SQRT_TWO_PI * (preact + 0.044715 * cubic)
    tangent = jnp.tanh(inner)
    activation = 0.5 * preact * (1.0 + tangent)
    slopes = 0.5 * (1.0 + tangent) + 0.5 * preact * (1.0 - tangent * tangent) * SQRT_TWO_PI * (
        1.0 + 3.0 * 0.044715 * preact * preact
    )
    return (activation, slopes)


def activate(core, keep, received, bias, cot, cot_other, piece, deps):
    tall, width = keep.shape
    half, reach = tall // 2, cot.shape[1] // 2

    def kernel(core_ref, keep_ref, received_ref, bias_ref, cot_ref, cot_other_ref, grad, act_mine, act_sent):
        cols = pl.ds(pl.multiple_of(core_ref[0] * reach + piece * width, 128), width)
        sides = ((core_ref[0], act_mine, cot_ref[:, cols]), (1 - core_ref[0], act_sent, cot_other_ref[:, cols]))
        for owner, act_ref, slope_cot in sides:
            rows = pl.ds(pl.multiple_of(owner * half, half), half)
            preact = keep_ref[rows, :].astype(F32) + received_ref[rows, :].astype(F32) + bias_ref[:, cols]
            act, slopes = gelu_parts(preact)
            grad[rows, :] = (slope_cot.astype(F32) * slopes).astype(BF16)
            act_ref[...] = act.astype(BF16)

    return local_call(
        kernel,
        [near_shape(tall, width), near_shape(half, width), near_shape(half, width)],
        [core, keep, received, bias, cot, cot_other],
        [SCALAR] + [WHOLE] * 5,
        deps,
        name="activate",
    )


def place_activation(core, mine, other, deps):
    rows, width = mine[0].shape
    reach = len(mine) * width

    def kernel(core_ref, *refs):
        *mine_refs, other_ref, out = refs
        for i, ref in enumerate(mine_refs):
            out[:, pl.ds(pl.multiple_of(core_ref[0] * reach + i * width, 128), width)] = ref[...]
            there = pl.ds(pl.multiple_of((1 - core_ref[0]) * reach + i * width, 128), width)
            out[:, there] = other_ref[i * rows : (i + 1) * rows, :]

    return local_call(
        kernel,
        shape(rows, 2 * reach),
        [core, *mine, other],
        [SCALAR] + [WHOLE] * (len(mine) + 1),
        deps,
        name="place_activation",
    )


def index_of(array, arrays):
    return [array is other for other in arrays].index(True)


def distinct(arrays):
    found = []
    for array in arrays:
        if not any(array is other for other in found):
            found.append(array)
    return found


def input_terms(weight, total, grads, deps, out_type=F32):
    arrays = [array for pair in grads.values() for array in pair]
    half, width = arrays[0].shape
    tall = 2 * half // BLOCKS
    pieces = list(grads)
    cols = slice(pieces[0] * width, (pieces[-1] + 1) * width)
    started = total is not None

    def kernel(*refs):
        total_ref, ins, weight_ref, out = refs[0], refs[started:-2], refs[-2], refs[-1]

        def rows_of(piece, block):
            spot = place(block, ROW_DIMS, ROW_ORDERS[piece % 3])
            return ins[pieces.index(piece) * 2 + spot // 4][spot % 4 * tall : (spot % 4 + 1) * tall, :]

        for chunk in range(2):
            blocks = range(chunk * 4, chunk * 4 + 4)
            left = jnp.concatenate(
                [jnp.concatenate([rows_of(piece, block) for block in blocks], axis=0) for piece in pieces], axis=1
            )
            term = lax.dot_general(left, weight_ref[:, cols], (((1,), (1,)), ((), ())), preferred_element_type=F32)
            rows = slice(chunk * half, (chunk + 1) * half)
            if started:
                term += total_ref[rows, :]
            out[rows, :] = term.astype(out_type)

    operands = ([total] if started else []) + arrays + [weight]
    out_shape = near_shape(2 * half, weight.shape[0], dtype=out_type)
    return local_call(kernel, out_shape, operands, [WHOLE] * len(operands), deps, name="input_terms")


def finish_input_terms(bits, total, received, deps):
    tokens, model = total.shape
    tall, third = tokens // BLOCKS, model // 3

    def kernel(bits_ref, total_ref, received_ref, *outs):
        for block in range(BLOCKS):
            source = pl.ds(pl.multiple_of((block ^ bits_ref[0]) * tall, tall), tall)
            rows = (total_ref[source, :] + received_ref[source, :].astype(F32)).astype(BF16)
            for i, order in enumerate(COL_ORDERS):
                spot = place(block, COL_DIMS, order)
                target = outs[i * 2 if spot >= 4 else i * 2 + 1]
                target[spot % 4 * tall : (spot % 4 + 1) * tall, :] = rows[:, i * third : (i + 1) * third]

    out_shape = [near_shape(tokens // 2, third)] * 6
    specs = [SCALAR, WHOLE, WHOLE]
    return local_call(kernel, out_shape, [bits, total, received], specs, deps, name="finish_input_terms")


def weight_terms(flipped, grads, deps, joined=False):
    pieces = list(grads)
    arrays = [array for pair in grads.values() for array in pair]
    model, width = flipped[0].shape[0], arrays[0].shape[1]

    def kernel(*refs):
        flipped_refs, grad_refs, outs = refs[:3], refs[3 : 3 + len(arrays)], refs[3 + len(arrays) :]
        for i, piece in enumerate(pieces):
            right = jnp.concatenate([grad_refs[2 * i][...], grad_refs[2 * i + 1][...]], axis=0)
            total = jnp.dot(flipped_refs[piece % 3][...], right, preferred_element_type=F32)
            if joined:
                outs[0][:, i * width : (i + 1) * width] = total.astype(BF16)
            else:
                outs[i][...] = total.astype(BF16)

    operands = [*flipped, *arrays]
    out_shape = [near_shape(model, width * len(pieces))] if joined else [near_shape(model, width)] * len(pieces)
    return local_call(kernel, out_shape, operands, [WHOLE] * len(operands), deps, "weight_terms")


def place_weight_terms(core, mine, others, so_far, cols, group, deps):
    model = mine[0].shape[0]
    n = len(mine) + len(others)

    def kernel(core_ref, *refs):
        out, sems = refs[-2:]
        copies, at = [], [group * (cols // 4)] * 2
        for i, ref in enumerate(refs[:n]):
            side = int(i >= len(mine))
            owner, width = 1 - core_ref[0] if side else core_ref[0], ref.shape[1]
            start = pl.multiple_of(owner * (cols // 2) + at[side], 128)
            at[side] += width
            copies.append(pltpu.make_async_copy(ref, out.at[:, pl.ds(start, width)], sems.at[i]))
        for copy in copies:
            copy.start()
        for copy in copies:
            copy.wait()

    operands = [core, *mine, *others, *deps] + ([] if so_far is None else [in_hbm(so_far)])
    return pl.pallas_call(
        kernel,
        out_shape=pltpu.HBM((model, cols), BF16),
        in_specs=[SCALAR] + [WHOLE] * n + [UNREAD] * (len(operands) - 1 - n),
        out_specs=UNREAD,
        scratch_shapes=[pltpu.SemaphoreType.DMA((n,))],
        input_output_aliases={} if so_far is None else {len(operands) - 1: 0},
        compiler_params=pltpu.CompilerParams(vmem_limit_bytes=8 * 2**20),
        cost_estimate=LIGHT,
        name="place_weight_terms",
    )(*operands)


def after(arrays, *deps):
    return list(lax.optimization_barrier((tuple(arrays), deps))[0])


def body(inputs, weight, hidden_bias, cotangent):
    row, col = lax.axis_index("row"), lax.axis_index("col")
    core = (row % 2).astype(jnp.int32)[None]
    cube = lambda ring, last: ((ring % 2) ^ (ring // 2)) * 4 + ring // 2 * 2 + last
    bits = (cube(row // 4, row // 2 % 2) ^ cube(col // 2, col % 2)).astype(jnp.int32)[None]
    hidden = weight.shape[1]
    width = hidden // 2 // PIECES
    sets = (range(0, 3), range(3, 6))
    bias = hidden_bias[None, :]

    third = inputs.shape[1] // 3
    parts = [inputs[:, i * third : (i + 1) * third] for i in range(3)]
    weight_there = swap(weight, "core")
    for turn in (2, 1):
        parts = after(gather_round(parts, COL_ORDERS, turn))
    received = [swap(part, order[0]) for part, order in zip(parts, COL_ORDERS)]
    parts = [stack(part, there, ()) for part, there in zip(parts, received)]
    parts_other = [swap(part, "core") for part in parts]
    weight_mine, weight_other = take_halves(core, [weight, weight_there], (parts[2],))
    mine = order_tokens(bits, parts, (weight_mine,))
    other = order_tokens(bits, parts_other, (mine,))
    cot_other = swap(after([cotangent], *parts)[0], "core")

    orders = [ROW_ORDERS[p % 3] for p in range(PIECES)]
    send, keep, last = [None] * PIECES, [None] * PIECES, ()
    for p in range(PIECES):
        send[p], keep[p] = project(mine, other, weight_mine, weight_other, p, width, last)
        last = (keep[p],)

    received = [None] * PIECES
    for turn in range(3):
        for p in range(PIECES):
            received[p] = swap(send[p], orders[p][turn])
        if turn < 2:
            for p in range(PIECES):
                send[p], keep[p] = add_halves(keep[p], received[p], last)
                last = (keep[p],)
            send = after(send[:3]) + after(send[3:])
    grads, act_mine, act_sent = [], [], []
    for p in range(PIECES):
        grad, a, b = activate(core, keep[p], received[p], bias, cotangent, cot_other, p, last)
        last = (grad,)
        grads.append(grad)
        act_mine.append(a)
        act_sent.append(b)

    flipped = transposed(mine, last)
    flipped_other = transposed(other, last)
    last = (flipped[0], flipped_other[0])
    for turn in (2, 1):
        received = [swap(grads[p], orders[p][turn]) for p in range(PIECES)]
        for p in range(PIECES):
            grads[p] = stack(grads[p], received[p], last)
            last = (grads[p],)
        grads = after(grads)
    first, second = sets
    arrived = [swap(grads[p], orders[p][0]) for p in range(PIECES)]
    ready = after([arrived[p] for p in first], grads[5])
    pairs = {p: (grads[p], ready[p]) for p in first}
    there = input_terms(weight_other, None, pairs, ())
    total = input_terms(weight_mine, None, pairs, (there,))
    sent = weight_terms(flipped_other, pairs, (total,), True)
    columns = {(0, 1): [swap(piece, "core") for piece in sent]}
    columns[0, 0] = weight_terms(flipped, pairs, (sent[0],))
    ready = after([arrived[p] for p in second], columns[0, 0][0])
    pairs = {p: (grads[p], ready[p - 3]) for p in second}
    there = input_terms(weight_other, there, pairs, (), BF16)
    received = swap(there, "core")
    sent = weight_terms(flipped_other, pairs, (there,), True)
    columns[1, 1] = [swap(sent[0], "core")]
    total = input_terms(weight_mine, total, pairs, (sent[0],))
    back = finish_input_terms(bits, total, received, ())

    send, keep = back[0::2], back[1::2]
    for turn in range(3):
        received = [swap(s, order[turn]) for s, order in zip(send, COL_ORDERS)]
        if turn == 0:
            columns[1, 0] = weight_terms(flipped, pairs, (keep[0],))
            done = (columns[1, 0][0],)
            weight_grad = place_weight_terms(core, columns[0, 0], columns[0, 1], None, hidden, 0, done)
        if turn == 1:
            act_other = swap(join(act_sent, (keep[0],)), "core")
            weight_grad = place_weight_terms(core, columns[1, 0], columns[1, 1], weight_grad, hidden, 1, (keep[0],))
        if turn < 2:
            sums = [add_halves(k, r, (in_hbm(weight_grad),)) for k, r in zip(keep, received)]
            send, keep = [a for a, _ in sums], [b for _, b in sums]
    activation = place_activation(core, act_mine, act_other, (keep[0],))
    input_grad = jnp.concatenate(
        [(k.astype(F32) + r.astype(F32)).astype(BF16) for k, r in zip(keep, received)], axis=1
    )
    return (activation, input_grad, weight_grad)


def solution(mesh):
    return jax.shard_map(
        body,
        mesh=mesh,
        in_specs=(P("col", "row"), P("row", "col"), P("col"), P("row", "col")),
        out_specs=(P("row", "col"), P("col", "row"), P("row", "col")),
        check_vma=False,
    )
```

```python
import math

import jax
import jax.numpy as jnp
from jax import lax
from jax.experimental import pallas as pl
from jax.experimental.pallas import tpu as pltpu
from jax.sharding import PartitionSpec as P

SQRT_TWO_PI = 0.7978845608028654
BF16, F32 = jnp.bfloat16, jnp.float32

N_ROW, N_COL = 16, 8
PIECES = 6
BLOCKS = 8
SPARE = 4 * 2**20

PAIRS = {
    "za": lambda z, h, c, x, l: (z ^ 1, h, c, x, l),
    "zb": lambda z, h, c, x, l: (3 - z, h, c, x, l),
    "yh": lambda z, h, c, x, l: (z, 1 - h, c, x, l),
    "xa": lambda z, h, c, x, l: (z, h, c, x ^ 1, l),
    "xb": lambda z, h, c, x, l: (z, h, c, 3 - x, l),
    "yl": lambda z, h, c, x, l: (z, h, c, x, 1 - l),
    "core": lambda z, h, c, x, l: (z, h, 1 - c, x, l),
}
ROW_DIMS, COL_DIMS = ("za", "zb", "yh"), ("xa", "xb", "yl")
ROW_ORDERS = (("za", "zb", "yh"), ("zb", "yh", "za"), ("yh", "za", "zb"))
COL_ORDERS = (("xa", "xb", "yl"), ("xb", "yl", "xa"), ("yl", "xa", "xb"))

WHOLE = pl.BlockSpec(memory_space=pltpu.VMEM)
UNREAD = pl.BlockSpec(memory_space=pl.ANY)
SCALAR = pl.BlockSpec(memory_space=pltpu.SMEM)
LIGHT = pl.CostEstimate(flops=0, bytes_accessed=1, transcendentals=0)


def pairing(dim):
    pairs = []
    for device in range(N_ROW * N_COL):
        row, col = divmod(device, N_COL)
        z, h, c, x, l = PAIRS[dim](row // 4, row // 2 % 2, row % 2, col // 2, col % 2)
        pairs.append((device, ((z * 2 + h) * 2 + c) * N_COL + x * 2 + l))
    return pairs


def swap(array, dim):
    return lax.ppermute(array, ("row", "col"), pairing(dim))


def place(block, dims, order):
    spot = 0
    for dim in order:
        spot = spot * 2 + ((block >> (len(dims) - 1 - dims.index(dim))) & 1)
    return spot


def local_call(kernel, out_shape, operands, specs, deps=(), name=None, **kw):
    n = len(operands)

    def run(*refs):
        kernel(*refs[:n], *refs[n + len(deps) :])

    outs = out_shape if isinstance(out_shape, list) else [out_shape]
    held = sum(math.prod(a.shape) * a.dtype.itemsize for a in list(operands) + outs)
    return pl.pallas_call(
        run,
        out_shape=out_shape,
        in_specs=list(specs) + [UNREAD] * len(deps),
        out_specs=[WHOLE] * len(out_shape) if isinstance(out_shape, list) else WHOLE,
        compiler_params=pltpu.CompilerParams(vmem_limit_bytes=held + SPARE),
        cost_estimate=LIGHT,
        name=name,
        **kw,
    )(*operands, *deps)


def shape(*dims, dtype=BF16):
    return jax.ShapeDtypeStruct(dims, dtype)


def near_shape(*dims, dtype=BF16):
    return pltpu.VMEM(dims, dtype)


def in_hbm(array):
    return pltpu.with_memory_space_constraint(array, pltpu.HBM)


def gather_round(blocks, orders, turn):
    others = [swap(block, order[turn]) for block, order in zip(blocks, orders)]
    return [jnp.concatenate(pair, axis=0) for pair in zip(blocks, others)]


def stack(near, far, deps):
    tall = near.shape[0]

    def kernel(near_ref, far_ref, out):
        out[:tall, :] = near_ref[...]
        out[tall:, :] = far_ref[...]

    return local_call(kernel, near_shape(2 * tall, near.shape[1]), [near, far], [WHOLE] * 2, deps, name="stack")


def join(arrays, deps):
    tall, width = arrays[0].shape

    def kernel(*refs):
        for i, ref in enumerate(refs[:-1]):
            refs[-1][i * tall : (i + 1) * tall, :] = ref[...]

    out_shape = near_shape(len(arrays) * tall, width)
    return local_call(kernel, out_shape, arrays, [WHOLE] * len(arrays), deps, name="join")


def take_halves(core, weights, deps):
    n = len(weights)
    model, reach = weights[0].shape[0], weights[0].shape[1] // 2

    def kernel(core_ref, *refs):
        outs, sems = refs[-1 - n : -1], refs[-1]
        start = pl.multiple_of(core_ref[0] * reach, reach)
        copies = [
            pltpu.make_async_copy(ref.at[:, pl.ds(start, reach)], out, sems.at[i])
            for i, (ref, out) in enumerate(zip(refs[:n], outs))
        ]
        for copy in copies:
            copy.start()
        for copy in copies:
            copy.wait()

    return pl.pallas_call(
        kernel,
        out_shape=[near_shape(model, reach)] * n,
        in_specs=[SCALAR] + [UNREAD] * (n + len(deps)),
        out_specs=[WHOLE] * n,
        scratch_shapes=[pltpu.SemaphoreType.DMA((n,))],
        compiler_params=pltpu.CompilerParams(vmem_limit_bytes=12 * 2**20),
        cost_estimate=LIGHT,
        name="take_halves",
    )(core, *[in_hbm(weight) for weight in weights], *deps)


def order_tokens(bits, parts, deps):
    tall, wide = parts[0].shape[0] // BLOCKS, parts[0].shape[1]

    def kernel(bits_ref, *refs):
        *part_refs, out = refs
        for block in range(BLOCKS):
            source = block ^ bits_ref[0]
            for i, part in enumerate(part_refs):
                spot = pl.multiple_of(place(source, COL_DIMS, COL_ORDERS[i]) * tall, tall)
                out[block * tall : (block + 1) * tall, i * wide : (i + 1) * wide] = part[pl.ds(spot, tall), :]

    out_shape = near_shape(BLOCKS * tall, wide * len(parts))
    return local_call(kernel, out_shape, [bits] + parts, [SCALAR] + [WHOLE] * len(parts), deps, name="order_tokens")


def transposed(tokens, deps):
    tall = tokens.shape[0] // BLOCKS

    def kernel(tokens_ref, *outs):
        for block in range(BLOCKS):
            flipped = tokens_ref[block * tall : (block + 1) * tall, :].T
            for order, out in zip(ROW_ORDERS, outs):
                spot = place(block, ROW_DIMS, order) * tall
                out[:, spot : spot + tall] = flipped

    out_shape = [near_shape(tokens.shape[1], tokens.shape[0])] * 3
    return local_call(kernel, out_shape, [tokens], [WHOLE], deps, name="transposed")


def project(mine, other, weight, weight_other, piece, width, deps):
    tokens = mine.shape[0]
    half, tall = tokens // 2, tokens // BLOCKS
    order = ROW_ORDERS[piece % 3]
    cols = slice(piece * width, (piece + 1) * width)

    def kernel(mine_ref, other_ref, near_ref, far_ref, send, keep):
        right = jnp.concatenate([near_ref[:, cols], far_ref[:, cols]], axis=0)
        for chunk in range(2):
            rows = slice(chunk * half, (chunk + 1) * half)
            left = jnp.concatenate([mine_ref[rows, :], other_ref[rows, :]], axis=1)
            total = jnp.dot(left, right, preferred_element_type=F32).astype(BF16)
            for i in range(4):
                spot = place(chunk * 4 + i, ROW_DIMS, order)
                target = send if spot >= 4 else keep
                target[spot % 4 * tall : (spot % 4 + 1) * tall, :] = total[i * tall : (i + 1) * tall]

    return local_call(
        kernel,
        [near_shape(half, width)] * 2,
        [mine, other, weight, weight_other],
        [WHOLE] * 4,
        deps,
        name="project",
    )


def add_halves(keep, received, deps):
    half = keep.shape[0] // 2

    def kernel(keep_ref, received_ref, send, kept):
        total = (keep_ref[...].astype(F32) + received_ref[...].astype(F32)).astype(BF16)
        kept[...] = total[:half]
        send[...] = total[half:]

    out_shape = [near_shape(half, keep.shape[1])] * 2
    return local_call(kernel, out_shape, [keep, received], [WHOLE] * 2, deps, name="add_halves")


def gelu_parts(preact):
    cubic = preact * preact * preact
    inner = SQRT_TWO_PI * (preact + 0.044715 * cubic)
    tangent = jnp.tanh(inner)
    activation = 0.5 * preact * (1.0 + tangent)
    slopes = 0.5 * (1.0 + tangent) + 0.5 * preact * (1.0 - tangent * tangent) * SQRT_TWO_PI * (
        1.0 + 3.0 * 0.044715 * preact * preact
    )
    return (activation, slopes)


def activate(core, keep, received, bias, cot, cot_other, piece, deps):
    tall, width = keep.shape
    half, reach = tall // 2, cot.shape[1] // 2

    def kernel(core_ref, keep_ref, received_ref, bias_ref, cot_ref, cot_other_ref, grad, act_mine, act_sent):
        cols = pl.ds(pl.multiple_of(core_ref[0] * reach + piece * width, 128), width)
        sides = ((core_ref[0], act_mine, cot_ref[:, cols]), (1 - core_ref[0], act_sent, cot_other_ref[:, cols]))
        for owner, act_ref, slope_cot in sides:
            rows = pl.ds(pl.multiple_of(owner * half, half), half)
            preact = keep_ref[rows, :].astype(F32) + received_ref[rows, :].astype(F32) + bias_ref[:, cols]
            act, slopes = gelu_parts(preact)
            grad[rows, :] = (slope_cot.astype(F32) * slopes).astype(BF16)
            act_ref[...] = act.astype(BF16)

    return local_call(
        kernel,
        [near_shape(tall, width), near_shape(half, width), near_shape(half, width)],
        [core, keep, received, bias, cot, cot_other],
        [SCALAR] + [WHOLE] * 5,
        deps,
        name="activate",
    )


def place_activation(core, mine, other, deps):
    rows, width = mine[0].shape
    reach = len(mine) * width

    def kernel(core_ref, *refs):
        *mine_refs, other_ref, out = refs
        for i, ref in enumerate(mine_refs):
            out[:, pl.ds(pl.multiple_of(core_ref[0] * reach + i * width, 128), width)] = ref[...]
            there = pl.ds(pl.multiple_of((1 - core_ref[0]) * reach + i * width, 128), width)
            out[:, there] = other_ref[i * rows : (i + 1) * rows, :]

    return local_call(
        kernel,
        shape(rows, 2 * reach),
        [core, *mine, other],
        [SCALAR] + [WHOLE] * (len(mine) + 1),
        deps,
        name="place_activation",
    )


def index_of(array, arrays):
    return [array is other for other in arrays].index(True)


def distinct(arrays):
    found = []
    for array in arrays:
        if not any(array is other for other in found):
            found.append(array)
    return found


def input_terms(weight, total, grads, deps, out_type=F32):
    arrays = [array for pair in grads.values() for array in pair]
    half, width = arrays[0].shape
    tall = 2 * half // BLOCKS
    pieces = list(grads)
    cols = slice(pieces[0] * width, (pieces[-1] + 1) * width)
    started = total is not None

    def kernel(*refs):
        total_ref, ins, weight_ref, out = refs[0], refs[started:-2], refs[-2], refs[-1]

        def rows_of(piece, block):
            spot = place(block, ROW_DIMS, ROW_ORDERS[piece % 3])
            return ins[pieces.index(piece) * 2 + spot // 4][spot % 4 * tall : (spot % 4 + 1) * tall, :]

        for chunk in range(2):
            blocks = range(chunk * 4, chunk * 4 + 4)
            left = jnp.concatenate(
                [jnp.concatenate([rows_of(piece, block) for block in blocks], axis=0) for piece in pieces], axis=1
            )
            term = lax.dot_general(left, weight_ref[:, cols], (((1,), (1,)), ((), ())), preferred_element_type=F32)
            rows = slice(chunk * half, (chunk + 1) * half)
            if started:
                term += total_ref[rows, :]
            out[rows, :] = term.astype(out_type)

    operands = ([total] if started else []) + arrays + [weight]
    out_shape = near_shape(2 * half, weight.shape[0], dtype=out_type)
    return local_call(kernel, out_shape, operands, [WHOLE] * len(operands), deps, name="input_terms")


def finish_input_terms(bits, total, received, deps):
    tokens, model = total.shape
    tall, third = tokens // BLOCKS, model // 3

    def kernel(bits_ref, total_ref, received_ref, *outs):
        for block in range(BLOCKS):
            source = pl.ds(pl.multiple_of((block ^ bits_ref[0]) * tall, tall), tall)
            rows = (total_ref[source, :] + received_ref[source, :].astype(F32)).astype(BF16)
            for i, order in enumerate(COL_ORDERS):
                spot = place(block, COL_DIMS, order)
                target = outs[i * 2 if spot >= 4 else i * 2 + 1]
                target[spot % 4 * tall : (spot % 4 + 1) * tall, :] = rows[:, i * third : (i + 1) * third]

    out_shape = [near_shape(tokens // 2, third)] * 6
    specs = [SCALAR, WHOLE, WHOLE]
    return local_call(kernel, out_shape, [bits, total, received], specs, deps, name="finish_input_terms")


def weight_terms(flipped, grads, deps, joined=False):
    pieces = list(grads)
    arrays = [array for pair in grads.values() for array in pair]
    model, width = flipped[0].shape[0], arrays[0].shape[1]

    def kernel(*refs):
        flipped_refs, grad_refs, outs = refs[:3], refs[3 : 3 + len(arrays)], refs[3 + len(arrays) :]
        for i, piece in enumerate(pieces):
            right = jnp.concatenate([grad_refs[2 * i][...], grad_refs[2 * i + 1][...]], axis=0)
            total = jnp.dot(flipped_refs[piece % 3][...], right, preferred_element_type=F32)
            if joined:
                outs[0][:, i * width : (i + 1) * width] = total.astype(BF16)
            else:
                outs[i][...] = total.astype(BF16)

    operands = [*flipped, *arrays]
    out_shape = [near_shape(model, width * len(pieces))] if joined else [near_shape(model, width)] * len(pieces)
    return local_call(kernel, out_shape, operands, [WHOLE] * len(operands), deps, "weight_terms")


def place_weight_terms(core, mine, others, so_far, cols, group, deps):
    model = mine[0].shape[0]
    n = len(mine) + len(others)

    def kernel(core_ref, *refs):
        out, sems = refs[-2:]
        copies, at = [], [group * (cols // 4)] * 2
        for i, ref in enumerate(refs[:n]):
            side = int(i >= len(mine))
            owner, width = 1 - core_ref[0] if side else core_ref[0], ref.shape[1]
            start = pl.multiple_of(owner * (cols // 2) + at[side], 128)
            at[side] += width
            copies.append(pltpu.make_async_copy(ref, out.at[:, pl.ds(start, width)], sems.at[i]))
        for copy in copies:
            copy.start()
        for copy in copies:
            copy.wait()

    operands = [core, *mine, *others, *deps] + ([] if so_far is None else [in_hbm(so_far)])
    return pl.pallas_call(
        kernel,
        out_shape=pltpu.HBM((model, cols), BF16),
        in_specs=[SCALAR] + [WHOLE] * n + [UNREAD] * (len(operands) - 1 - n),
        out_specs=UNREAD,
        scratch_shapes=[pltpu.SemaphoreType.DMA((n,))],
        input_output_aliases={} if so_far is None else {len(operands) - 1: 0},
        compiler_params=pltpu.CompilerParams(vmem_limit_bytes=8 * 2**20),
        cost_estimate=LIGHT,
        name="place_weight_terms",
    )(*operands)


def after(arrays, *deps):
    return list(lax.optimization_barrier((tuple(arrays), deps))[0])


def body(inputs, weight, hidden_bias, cotangent):
    row, col = lax.axis_index("row"), lax.axis_index("col")
    core = (row % 2).astype(jnp.int32)[None]
    cube = lambda ring, last: ((ring % 2) ^ (ring // 2)) * 4 + ring // 2 * 2 + last
    bits = (cube(row // 4, row // 2 % 2) ^ cube(col // 2, col % 2)).astype(jnp.int32)[None]
    hidden = weight.shape[1]
    width = hidden // 2 // PIECES
    sets = (range(0, 3), range(3, 6))
    bias = hidden_bias[None, :]

    third = inputs.shape[1] // 3
    parts = [inputs[:, i * third : (i + 1) * third] for i in range(3)]
    weight_there = swap(weight, "core")
    for turn in (2, 1):
        parts = after(gather_round(parts, COL_ORDERS, turn))
    received = [swap(part, order[0]) for part, order in zip(parts, COL_ORDERS)]
    parts = [stack(part, there, ()) for part, there in zip(parts, received)]
    parts_other = [swap(part, "core") for part in parts]
    weight_mine, weight_other = take_halves(core, [weight, weight_there], (parts[2],))
    mine = order_tokens(bits, parts, (weight_mine,))
    other = order_tokens(bits, parts_other, (mine,))
    cot_other = swap(after([cotangent], *parts)[0], "core")

    orders = [ROW_ORDERS[p % 3] for p in range(PIECES)]
    send, keep, last = [None] * PIECES, [None] * PIECES, ()
    for p in range(PIECES):
        send[p], keep[p] = project(mine, other, weight_mine, weight_other, p, width, last)
        last = (keep[p],)

    received = [None] * PIECES
    for turn in range(3):
        for p in range(PIECES):
            received[p] = swap(send[p], orders[p][turn])
        if turn < 2:
            for p in range(PIECES):
                send[p], keep[p] = add_halves(keep[p], received[p], last)
                last = (keep[p],)
            send = after(send[:3]) + after(send[3:])
    grads, act_mine, act_sent = [], [], []
    for p in range(PIECES):
        grad, a, b = activate(core, keep[p], received[p], bias, cotangent, cot_other, p, last)
        last = (grad,)
        grads.append(grad)
        act_mine.append(a)
        act_sent.append(b)

    flipped = transposed(mine, last)
    flipped_other = transposed(other, last)
    last = (flipped[0], flipped_other[0])
    for turn in (2, 1):
        received = [swap(grads[p], orders[p][turn]) for p in range(PIECES)]
        for p in range(PIECES):
            grads[p] = stack(grads[p], received[p], last)
            last = (grads[p],)
        grads = after(grads)
    first, second = sets
    arrived = [swap(grads[p], orders[p][0]) for p in range(PIECES)]
    ready = after([arrived[p] for p in first], grads[5])
    pairs = {p: (grads[p], ready[p]) for p in first}
    there = input_terms(weight_other, None, pairs, ())
    total = input_terms(weight_mine, None, pairs, (there,))
    sent = weight_terms(flipped_other, pairs, (total,), True)
    columns = {(0, 1): [swap(piece, "core") for piece in sent]}
    columns[0, 0] = weight_terms(flipped, pairs, (sent[0],))
    ready = after([arrived[p] for p in second], columns[0, 0][0])
    pairs = {p: (grads[p], ready[p - 3]) for p in second}
    there = input_terms(weight_other, there, pairs, (), BF16)
    received = swap(there, "core")
    total = input_terms(weight_mine, total, pairs, (there,))
    sent = weight_terms(flipped_other, pairs, (total, received), True)
    columns[1, 1] = [swap(sent[0], "core")]
    back = finish_input_terms(bits, total, received, ())

    send, keep = back[0::2], back[1::2]
    for turn in range(3):
        received = [swap(s, order[turn]) for s, order in zip(send, COL_ORDERS)]
        if turn == 0:
            columns[1, 0] = weight_terms(flipped, pairs, (keep[0],))
            done = (columns[1, 0][0],)
            weight_grad = place_weight_terms(core, columns[0, 0], columns[0, 1], None, hidden, 0, done)
        if turn == 1:
            act_other = swap(join(act_sent, (keep[0],)), "core")
            weight_grad = place_weight_terms(core, columns[1, 0], columns[1, 1], weight_grad, hidden, 1, (keep[0],))
        if turn < 2:
            sums = [add_halves(k, r, (in_hbm(weight_grad),)) for k, r in zip(keep, received)]
            send, keep = [a for a, _ in sums], [b for _, b in sums]
    activation = place_activation(core, act_mine, act_other, (keep[0],))
    input_grad = jnp.concatenate(
        [(k.astype(F32) + r.astype(F32)).astype(BF16) for k, r in zip(keep, received)], axis=1
    )
    return (activation, input_grad, weight_grad)


def solution(mesh):
    return jax.shard_map(
        body,
        mesh=mesh,
        in_specs=(P("col", "row"), P("row", "col"), P("col"), P("row", "col")),
        out_specs=(P("row", "col"), P("col", "row"), P("row", "col")),
        check_vma=False,
    )
```
